256 devices in a mesh: blk: 32 (over x, z_hi, y), head: 8 (over z_lo, core).
Axes of the slice: x: 4, y: 4, z: 8 (z_hi: 2, z_lo: 4; z = z_hi * 4 + z_lo), core: 2. Of those that a mesh axis runs over, the one named last changes fastest.
Arguments:
- queries: bfloat16 [2048, 64, 128], P(('blk', 'head')), may hold values from -12 to 12
- text_keyval: bfloat16 [32768, 8, 2, 128], P(('blk', 'head')), may hold values from -6 to 6
- visual_keyval: bfloat16 [12288, 8, 2, 128], P(('blk', 'head')), may hold values from -6 to 6
- visual_counts: int32 [256], replicated, may hold values from 1 to 95, as said below
Outputs:
- attended: bfloat16 [2048, 64, 128], P(('blk', 'head'))
The draws below stay inside these ranges and needn't reach their ends.
Inputs may be any that keep to these rules, and one draw needn't show every extreme that they name: `visual_counts`: with d[o] = offsets[o + 1] - (o + 1) * 48: 0 <= d[o] < 48 for every device o, d of the next-to-last device is 47, d of the last device is 0, so the counts sum to 12288 and a device's visual rows lie in the visual blocks of itself and the next device.
All inputs are finite; a program needn't handle non-finite values.
Results may differ from the reference program's by a relative error of at most 0.018.
Values may be sent and summed in bfloat16 or wider, within the bound.
No kernel may reach another device: no remote copies, remote signals or barrier semaphores. Data moves between devices by JAX's collectives and lax.ppermute only.
A program may use at most 64 MiB of HBM per device.

```python
import math
import jax
import jax.numpy as jnp
from jax import lax

Q_HEADS = 64
KV_HEADS = 8
HEAD_DIM = 128
TOK_DEV = 128
QB = 8
VIS_DEV = 48
OWNERS = 256
TOKENS = 32768
VISUAL = 12288
QUERIES = 2048


def plant_pattern(key):
    return jnp.where(jax.random.bernoulli(key, 0.5, (KV_HEADS, HEAD_DIM)), 1.0, -1.0)


def aligned_pattern(key):
    half_sign = jnp.where(jnp.arange(HEAD_DIM, dtype=jnp.int32) < HEAD_DIM // 2, 1.0, -1.0)
    return plant_pattern(key) * half_sign[None, :]


def draw_queries(key, part):
    aligned = aligned_pattern(key)
    key = jax.random.fold_in(key, 11)
    shape = (QUERIES, Q_HEADS, HEAD_DIM)
    row_order = jnp.arange(QUERIES, dtype=jnp.int32)
    values_drawn = jnp.clip(3.0 * jax.random.normal(key, shape, jnp.float32), -12.0, 12.0)
    target = row_order == (OWNERS - 2) * QB + QB - 1
    aligned_wide = 4.0 * jnp.repeat(aligned, Q_HEADS // KV_HEADS, axis=0)
    values_drawn = jnp.where(target[:, None, None], aligned_wide[None, :, :], values_drawn)
    return values_drawn.astype(jnp.bfloat16)


def draw_text_keyval(key, part):
    key = jax.random.fold_in(key, 23)
    shape = (TOKENS, KV_HEADS, 2, HEAD_DIM)
    values_drawn = jnp.clip(jax.random.normal(key, shape, jnp.float32), -6.0, 6.0)
    return values_drawn.astype(jnp.bfloat16)


def draw_visual_keyval(key, part):
    aligned = aligned_pattern(key)
    key = jax.random.fold_in(key, 37)
    shape = (VISUAL, KV_HEADS, 2, HEAD_DIM)
    values_drawn = jnp.clip(jax.random.normal(key, shape, jnp.float32), -6.0, 6.0)
    row_order = jnp.arange(VISUAL, dtype=jnp.int32)
    chosen = (row_order >= (OWNERS - 1) * VIS_DEV) & (row_order < OWNERS * VIS_DEV - 1)
    key_part = jnp.where(chosen[:, None, None], 5.0 * aligned[None, :, :], values_drawn[:, :, 0, :])
    values_drawn = jnp.stack([key_part, values_drawn[:, :, 1, :]], axis=2)
    return values_drawn.astype(jnp.bfloat16)


def draw_visual_counts(key, part):
    key = jax.random.fold_in(key, 5)
    device_order = jnp.arange(OWNERS, dtype=jnp.int32)
    drift_rows = jax.random.randint(key, (OWNERS,), 0, VIS_DEV, dtype=jnp.int32)
    drift_rows = jnp.where(device_order == 0, VIS_DEV - 1, drift_rows)
    drift_rows = jnp.where(device_order == 1, 0, drift_rows)
    drift_rows = jnp.where(device_order == OWNERS - 2, VIS_DEV - 1, drift_rows)
    drift_rows = jnp.where(device_order == OWNERS - 1, 0, drift_rows)
    earlier = jnp.concatenate([jnp.zeros((1,), jnp.int32), drift_rows[:-1]])
    return (VIS_DEV + drift_rows - earlier).astype(jnp.int32)


def setup_inputs(seed: int = 0) -> dict:
    seeds = jax.random.split(jax.random.key(seed), 5)
    queries = draw_queries(jax.random.fold_in(seeds[4], 71), 0)
    text_keyval = draw_text_keyval(jax.random.fold_in(seeds[4], 71), 0)
    visual_keyval = draw_visual_keyval(jax.random.fold_in(seeds[4], 71), 0)
    visual_counts = draw_visual_counts(jax.random.fold_in(seeds[4], 71), 0)
    return {"queries": queries, "text_keyval": text_keyval, "visual_keyval": visual_keyval, "visual_counts": visual_counts}


def reference(queries, text_keyval, visual_keyval, visual_counts):
    offsets = jnp.cumsum(visual_counts) - visual_counts
    positions = jnp.arange(TOKENS, dtype=jnp.int32)
    owner_index = positions // TOK_DEV
    row_within = positions % TOK_DEV
    source_row = jnp.clip(offsets[owner_index] + row_within, 0, VISUAL - 1).astype(jnp.int32)
    is_visual = row_within < visual_counts[owner_index]
    keyval = jnp.where(is_visual[:, None, None, None], visual_keyval[source_row], text_keyval)
    query_index = jnp.arange(QUERIES, dtype=jnp.int32)
    query_place = query_index // QB * TOK_DEV + TOK_DEV - QB + query_index % QB
    allowed = positions[None, :] <= query_place[:, None]
    group_size = Q_HEADS // KV_HEADS
    score_scale = 1.0 / math.sqrt(HEAD_DIM)

    def one_head(head_index):
        kv_index = head_index // group_size
        key_part = jnp.take(keyval[:, :, 0, :], kv_index, axis=1)
        value_part = jnp.take(keyval[:, :, 1, :], kv_index, axis=1)
        query_part = jnp.take(queries, head_index, axis=1)
        scores = jnp.dot(query_part, key_part.T, preferred_element_type=jnp.float32) * score_scale
        scores = jnp.where(allowed, scores, -1e+30)
        maxima = lax.optimization_barrier(jnp.max(scores, axis=1, keepdims=True))
        exponent = jnp.exp(scores - maxima)
        totals = lax.optimization_barrier(jnp.sum(exponent, axis=1, keepdims=True))
        weights = exponent.astype(jnp.bfloat16)
        summed = jnp.dot(weights, value_part, preferred_element_type=jnp.float32)
        return (summed / totals).astype(jnp.bfloat16)
    attended = lax.map(one_head, jnp.arange(Q_HEADS, dtype=jnp.int32))
    return jnp.transpose(attended, (1, 0, 2))
```

```python
import functools
import math

import jax
import jax.numpy as jnp
from jax import lax
from jax.experimental import pallas as pl
from jax.experimental.pallas import tpu as pltpu
from jax.sharding import Mesh, PartitionSpec as P

AXES = ("x", "zh", "y", "k", "zp", "c")
SIZES = (4, 2, 4, 2, 2, 2)
KEY_GROUP = ("x", "y", "zp")
QUERY_GROUP = ("x", "zh", "k", "zp")
NEVER = -1e30
VMEM = pl.BlockSpec(memory_space=pltpu.VMEM)


def place_kernel(counts_ref, text_ref, vis_ref, next_ref, send_ref, stacked):
    tok_rows = text_ref.shape[0] // 16
    vis_rows = vis_ref.shape[0] // 16
    owner = 0
    for axis, size in zip(AXES, SIZES):
        owner = owner * size + lax.axis_index(axis)
    counts = counts_ref[...].astype(jnp.float32)
    order = lax.broadcasted_iota(jnp.int32, counts.shape, 0) * 128 + lax.broadcasted_iota(
        jnp.int32, counts.shape, 1
    )
    before = jnp.sum(jnp.where(order < owner, counts, 0.0)).astype(jnp.int32)
    here = jnp.sum(jnp.where(order == owner, counts, 0.0)).astype(jnp.int32)
    start = jnp.clip(before - owner * vis_rows, 0, vis_rows - 1)
    stacked[0 : vis_rows * 16] = vis_ref[...]
    stacked[vis_rows * 16 : vis_rows * 32] = next_ref[...]
    out_row = lax.broadcasted_iota(jnp.int32, (256, 256), 0)
    in_row = lax.broadcasted_iota(jnp.int32, (256, 256), 1)
    to_heads = jnp.where(in_row == (out_row % 16) * 16 + out_row // 16, 1.0, 0.0)
    to_heads = to_heads.astype(jnp.bfloat16)
    row_within = lax.broadcasted_iota(jnp.int32, (256, 128), 0) // 16
    for part in range(tok_rows // 16):
        data = text_ref[part * 256 : (part + 1) * 256]
        if part * 16 < vis_rows * 2:
            window = stacked[pl.ds(pl.multiple_of(start * 16 + part * 256, 16), 256)]
            data = jnp.where(
                row_within + part * 16 < here, window.astype(jnp.float32), data.astype(jnp.float32)
            ).astype(jnp.bfloat16)
        moved = jnp.dot(to_heads, data, preferred_element_type=jnp.float32).astype(jnp.bfloat16)
        for head in range(8):
            for kind in range(2):
                slab = moved[(head * 2 + kind) * 16 : (head * 2 + kind + 1) * 16]
                for y in range(4):
                    send_ref[head // 2, y, head % 2, kind, part * 16 : (part + 1) * 16] = slab


def query_kernel(q_ref, send_ref):
    for pair in range(4):
        both = q_ref[:, pair * 16 : (pair + 1) * 16, :].astype(jnp.float32)
        for zp in range(2):
            chunk = both[:, zp * 8 : (zp + 1) * 8, :].reshape(64, 128).astype(jnp.bfloat16)
            for zh in range(2):
                for k in range(2):
                    send_ref[pair, zh, k, zp] = chunk


ROWS = 256


def attend_kernel(last, *refs):
    if last:
        q_ref, kv_ref, acc_in, m_in, send_ref = refs
    else:
        q_ref, kv_ref, acc_ref, m_ref = refs
    me = {axis: lax.axis_index(axis) for axis in ("zh", "y", "k", "c")}
    other = 1 - me["c"] if last else me["c"]
    scale = math.log2(math.e) / math.sqrt(128)
    ones = jnp.ones((1024, 128), jnp.bfloat16)

    def tile(xq, step):
        first = step * ROWS
        rows = pl.ds(pl.multiple_of(xq * 512 + first, ROWS), ROWS)
        scaled = q_ref[rows].astype(jnp.float32) * scale
        high = scaled.astype(jnp.bfloat16)
        low = (scaled - high.astype(jnp.float32)).astype(jnp.bfloat16)
        query = jnp.concatenate([high, low], axis=1)
        row = lax.broadcasted_iota(jnp.int32, (ROWS, 128), 0) + first
        lane = lax.broadcasted_iota(jnp.int32, (ROWS, 128), 1)
        z = row // 64
        q_dev = (z // 4) * 32 + me["y"] * 8 + ((z // 2) % 2) * 4 + (z % 2) * 2 + me["c"]
        reach = q_dev * 128 + 120 + (row % 64) // 8 - lane
        if last:
            maxima, acc = m_in[rows], acc_in[rows]
        for xk in range(xq + 1):
            keys = kv_ref[xk * 8 : (xk + 1) * 8, 0].reshape(1024, 128)
            values = kv_ref[xk * 8 : (xk + 1) * 8, 1].reshape(1024, 128)
            scores = lax.dot_general(
                query,
                jnp.concatenate([keys, keys], axis=1),
                (((1,), (1,)), ((), ())),
                preferred_element_type=jnp.float32,
            )
            parts = [scores[:, j * 128 : (j + 1) * 128] for j in range(8)]
            if xk == xq:
                for j in range(8):
                    k_dev = me["zh"] * 32 + (j // 2) * 8 + me["k"] * 4 + (j % 2) * 2 + other
                    parts[j] = jnp.where(reach >= k_dev * 128, parts[j], NEVER)
            top = functools.reduce(jnp.maximum, parts)
            top = jnp.max(top, axis=1, keepdims=True)
            if xk == 0 and not last:
                new = jnp.broadcast_to(top, (ROWS, 128))
            else:
                new = jnp.maximum(maxima, top)
            weights = jnp.concatenate(
                [jnp.exp2(part - new).astype(jnp.bfloat16) for part in parts], axis=1
            )
            added = jnp.dot(
                weights,
                jnp.concatenate([values, ones], axis=1),
                preferred_element_type=jnp.float32,
            )
            if xk == 0 and not last:
                acc = added
            else:
                shrink = jnp.exp2(maxima - new)
                acc = acc * jnp.concatenate([shrink, shrink], axis=1) + added
            maxima = new
        if not last:
            m_ref[rows] = maxima
            acc_ref[rows] = acc
            return
        totals = acc[:, 128:]
        result = (acc[:, :128] / totals).astype(jnp.bfloat16)
        level = maxima + jnp.log2(totals)
        eye = lax.broadcasted_iota(jnp.int32, (64, 128), 0) == lax.broadcasted_iota(
            jnp.int32, (64, 128), 1
        )
        stat_row = lax.broadcasted_iota(jnp.int32, (16, 128), 0)
        for j in range(ROWS // 64):
            chunk = xq * 8 + step * (ROWS // 64) + j
            send_ref[chunk, :64] = result[j * 64 : (j + 1) * 64]
            line = jnp.sum(
                jnp.where(eye, level[j * 64 : (j + 1) * 64], 0.0), axis=0, keepdims=True
            )
            one = line.astype(jnp.bfloat16).astype(jnp.float32)
            two = (line - one).astype(jnp.bfloat16).astype(jnp.float32)
            three = line - one - two
            stats = jnp.where(
                stat_row == 0, one, jnp.where(stat_row == 1, two, jnp.where(stat_row == 2, three, 0.0))
            )
            send_ref[chunk, 64:80] = stats.astype(jnp.bfloat16)

    for xq in range(4):
        @pl.loop(0, 512 // ROWS)
        def _(step):
            tile(xq, step)


def combine_kernel(recv_ref, out_ref):
    eye = lax.broadcasted_iota(jnp.int32, (64, 128), 0) == lax.broadcasted_iota(
        jnp.int32, (64, 128), 1
    )
    for x in range(4):
        heads = []
        for zp in range(2):
            chunks = [x * 8 + part * 2 + zp for part in range(4)]
            levels = []
            for chunk in chunks:
                stats = recv_ref[chunk, 64:80].astype(jnp.float32)
                levels.append(stats[0:1] + stats[1:2] + stats[2:3])
            top = functools.reduce(jnp.maximum, levels)
            shares = [jnp.exp2(level - top) for level in levels]
            whole = functools.reduce(jnp.add, shares)
            total = None
            for chunk, share in zip(chunks, shares):
                column = jnp.sum(jnp.where(eye, share / whole, 0.0), axis=1, keepdims=True)
                term = recv_ref[chunk, :64].astype(jnp.float32) * column
                total = term if total is None else total + term
            heads.append(total.reshape(8, 8, 128))
        out_ref[:, x * 16 : (x + 1) * 16, :] = jnp.concatenate(heads, axis=1).astype(jnp.bfloat16)


def params():
    return pltpu.CompilerParams(vmem_limit_bytes=32 * 1024 * 1024)


def on_device(queries, text_keyval, visual_keyval, visual_counts):
    owners = math.prod(SIZES)
    following = lax.ppermute(visual_keyval, AXES, [(i, i - 1) for i in range(1, owners)])
    q_send = pl.pallas_call(
        query_kernel,
        out_shape=jax.ShapeDtypeStruct((4, 2, 2, 2, 64, 128), jnp.bfloat16),
        in_specs=[VMEM],
        out_specs=VMEM,
        compiler_params=params(),
        name="query_chunks",
    )(queries)
    q_all = lax.all_to_all(q_send.reshape(32, 64, 128), QUERY_GROUP, 0, 0, tiled=True)
    q_all = q_all.reshape(2048, 128)
    kv_send = pl.pallas_call(
        place_kernel,
        out_shape=jax.ShapeDtypeStruct((4, 4, 2, 2, 128, 128), jnp.bfloat16),
        in_specs=[VMEM] * 4,
        out_specs=VMEM,
        scratch_shapes=[pltpu.VMEM((48 * 3 * 16, 128), jnp.bfloat16)],
        compiler_params=params(),
        name="place_rows",
    )(
        visual_counts.reshape(2, 128),
        text_keyval.reshape(2048, 128),
        visual_keyval.reshape(768, 128),
        following.reshape(768, 128),
    )
    kv_own = lax.all_to_all(kv_send.reshape(32, 2, 128, 128), KEY_GROUP, 0, 0, tiled=True)
    kv_other = lax.ppermute(kv_own, "c", [(0, 1), (1, 0)])
    acc, maxima = pl.pallas_call(
        functools.partial(attend_kernel, False),
        out_shape=(
            jax.ShapeDtypeStruct((2048, 256), jnp.float32),
            jax.ShapeDtypeStruct((2048, 128), jnp.float32),
        ),
        in_specs=[VMEM] * 2,
        out_specs=(VMEM, VMEM),
        compiler_params=params(),
        cost_estimate=pl.CostEstimate(
            flops=4 * 5242880 * 256, bytes_accessed=6 * 2**20, transcendentals=5242880
        ),
        name="attend_first",
    )(q_all, kv_own)
    o_send = pl.pallas_call(
        functools.partial(attend_kernel, True),
        out_shape=jax.ShapeDtypeStruct((32, 80, 128), jnp.bfloat16),
        in_specs=[VMEM] * 4,
        out_specs=VMEM,
        compiler_params=params(),
        name="attend_last",
    )(q_all, kv_other, acc, maxima)
    o_recv = lax.all_to_all(o_send, QUERY_GROUP, 0, 0, tiled=True)
    return pl.pallas_call(
        combine_kernel,
        out_shape=jax.ShapeDtypeStruct((8, 64, 128), jnp.bfloat16),
        in_specs=[VMEM],
        out_specs=VMEM,
        compiler_params=params(),
        name="combine_parts",
    )(o_recv)


def solution(mesh):
    fine = Mesh(mesh.devices.reshape(SIZES), AXES)
    in_specs = (
        P(AXES, None, None),
        P(AXES, None, None, None),
        P(AXES, None, None, None),
        P(),
    )
    out_specs = P(AXES, None, None)
    return jax.shard_map(
        on_device, mesh=fine, in_specs=in_specs, out_specs=out_specs, check_vma=False
    )
```

```python
import functools
import math

import jax
import jax.numpy as jnp
from jax import lax
from jax.experimental import pallas as pl
from jax.experimental.pallas import tpu as pltpu
from jax.sharding import Mesh, PartitionSpec as P

AXES = ("x", "zh", "y", "k", "zp", "c")
SIZES = (4, 2, 4, 2, 2, 2)
QUERY_GROUP = ("x", "zh", "k", "zp")
NEVER = -1e30
VMEM = pl.BlockSpec(memory_space=pltpu.VMEM)
SMEM = pl.BlockSpec(memory_space=pltpu.SMEM)


def head_order():
    out_row = lax.broadcasted_iota(jnp.int32, (256, 256), 0)
    in_row = lax.broadcasted_iota(jnp.int32, (256, 256), 1)
    moves = jnp.where(in_row == (out_row % 16) * 16 + out_row // 16, 1.0, 0.0)
    return moves.astype(jnp.bfloat16)


def local_kernel(
    counts_ref, q_ref, text_ref, vis_ref, q_out_ref, moved_ref, vis_out_ref, window_ref
):
    owner = 0
    for axis, size in zip(AXES, SIZES):
        owner = owner * size + lax.axis_index(axis)
    counts = counts_ref[...].astype(jnp.float32)
    order = lax.broadcasted_iota(jnp.int32, counts.shape, 0) * 128 + lax.broadcasted_iota(
        jnp.int32, counts.shape, 1
    )
    before = jnp.sum(jnp.where(order < owner, counts, 0.0)).astype(jnp.int32)
    here = jnp.sum(jnp.where(order == owner, counts, 0.0)).astype(jnp.int32)
    window_ref[0] = jnp.clip(before - owner * 48, 0, 47)
    window_ref[1] = here
    for pair in range(4):
        both = q_ref[:, pair * 16 : (pair + 1) * 16, :].astype(jnp.float32)
        for zp in range(2):
            chunk = both[:, zp * 8 : (zp + 1) * 8, :].reshape(64, 128)
            q_out_ref[pair * 2 + zp] = chunk.astype(jnp.bfloat16)
    vis_out_ref[...] = vis_ref[...]
    moves = head_order()
    for part in range(8):
        rows = slice(part * 256, (part + 1) * 256)
        moved_ref[rows] = jnp.dot(
            moves, text_ref[rows], preferred_element_type=jnp.float32
        ).astype(jnp.bfloat16)


def scale_kernel(mine_ref, near_ref, across_ref, far_ref, out_ref):
    scale = math.log2(math.e) / math.sqrt(128)
    for xq in range(4):
        rows = slice(xq * 128, (xq + 1) * 128)
        sets = [ref[rows] for ref in (mine_ref, near_ref, across_ref, far_ref)]
        scaled = jnp.concatenate(sets, axis=0).astype(jnp.float32) * scale
        high = scaled.astype(jnp.bfloat16)
        low = (scaled - high.astype(jnp.float32)).astype(jnp.bfloat16)
        out_ref[xq * 512 : (xq + 1) * 512] = jnp.concatenate([high, low], axis=1)


def place_kernel(window_ref, q_ref, moved_ref, vis_ref, next_ref, send_ref, stacked):
    send_ref[:, 256:320] = q_ref[...]
    start = window_ref[0]
    here = window_ref[1]
    stacked[0:768] = vis_ref[...]
    stacked[768:1536] = next_ref[...]
    stacked[1536:2304] = jnp.zeros((768, 128), jnp.bfloat16)
    moves = head_order()
    row_within = lax.broadcasted_iota(jnp.int32, (256, 128), 0) % 16
    for part in range(8):
        data = moved_ref[part * 256 : (part + 1) * 256]
        if part < 6:
            first = pl.multiple_of(start * 16 + part * 256, 16)
            window = jnp.dot(moves, stacked[pl.ds(first, 256)], preferred_element_type=jnp.float32)
            data = jnp.where(row_within + part * 16 < here, window, data.astype(jnp.float32))
            data = data.astype(jnp.bfloat16)
        for head in range(8):
            for kind in range(2):
                slab = data[(head * 2 + kind) * 16 : (head * 2 + kind + 1) * 16]
                first_row = kind * 128 + part * 16
                send_ref[head, first_row : first_row + 16] = slab


ROWS = 512


def attend_kernel(steps, swapped, shared, first, last, q_ref, *refs):
    refs = list(refs)
    kv_refs = [refs.pop(0) for _ in range(1 if shared else 2)]
    if shared:
        kv_refs = [kv_refs[0].at[0:8], kv_refs[0].at[8:16]]
    if not first:
        acc_in, m_in = refs[:2]
        refs = refs[2:]
    if last:
        (send_ref,) = refs
    else:
        acc_ref, m_ref = refs
    me = {axis: lax.axis_index(axis) for axis in ("zh", "y", "k", "c")}
    width = 512
    y = (me["y"] + steps[0] + steps[1] * me["c"]) % 4
    ones = jnp.ones((width, 128), jnp.bfloat16)
    row = lax.broadcasted_iota(jnp.int32, (ROWS, 128), 0)
    lane = lax.broadcasted_iota(jnp.int32, (ROWS, 128), 1)
    pair = me["zh"] * 2 + me["k"]
    turns = (0, 3 - 2 * me["c"], 2, 1 + 2 * me["c"])
    turn = functools.reduce(
        lambda so_far, j: jnp.where(row // 128 == j, turns[j], so_far), range(1, 4), row * 0
    )
    z = (pair + turn) % 4
    q_dev = (z // 2) * 32 + me["y"] * 8 + (z % 2) * 4 + (row // 64 % 2) * 2 + me["c"]
    reach = q_dev * 128 + 120 + (row % 64) // 8 - lane
    queries, state = {}, {}
    for xq in range(4):
        rows = slice(xq * ROWS, (xq + 1) * ROWS)
        queries[xq] = q_ref[rows]
        state[xq] = None if first else (m_in[rows], acc_in[rows])

    def gathered(xk, kind):
        found = []
        for kv_ref in kv_refs:
            rows = kv_ref[xk * 2 : xk * 2 + 2, kind * 128 : (kind + 1) * 128]
            found.append(rows.reshape(256, 128))
        return jnp.concatenate(found, axis=0)

    def score(xq, xk):
        keys = gathered(xk, 0)
        return lax.dot_general(
            queries[xq],
            jnp.concatenate([keys, keys], axis=1),
            (((1,), (1,)), ((), ())),
            preferred_element_type=jnp.float32,
        )

    def absorb(xq, xk, scores):
        parts = [scores[:, j * 128 : (j + 1) * 128] for j in range(width // 128)]
        if xk == xq:
            for j in range(width // 128):
                core = me["c"] if j // 2 == swapped else 1 - me["c"]
                k_dev = me["zh"] * 32 + y * 8 + me["k"] * 4 + j % 2 * 2 + core
                parts[j] = jnp.where(reach >= k_dev * 128, parts[j], NEVER)
        top = jnp.max(functools.reduce(jnp.maximum, parts), axis=1, keepdims=True)
        if state[xq] is None:
            new = jnp.broadcast_to(top, (ROWS, 128))
        else:
            new = jnp.maximum(state[xq][0], top)
        weights = jnp.concatenate(
            [jnp.exp2(part - new).astype(jnp.bfloat16) for part in parts], axis=1
        )
        values = gathered(xk, 1)
        acc = jnp.dot(
            weights, jnp.concatenate([values, ones], axis=1), preferred_element_type=jnp.float32
        )
        if state[xq] is not None:
            shrink = jnp.exp2(state[xq][0] - new)
            acc = state[xq][1] * jnp.concatenate([shrink, shrink], axis=1) + acc
        state[xq] = (new, acc)

    def finish(xq):
        maxima, acc = state[xq]
        if not last:
            m_ref[xq * ROWS : (xq + 1) * ROWS] = maxima
            acc_ref[xq * ROWS : (xq + 1) * ROWS] = acc
            return
        totals = acc[:, 128:]
        result = (acc[:, :128] / totals).astype(jnp.bfloat16)
        level = maxima + jnp.log2(totals)
        eye = lax.broadcasted_iota(jnp.int32, (64, 128), 0) == lax.broadcasted_iota(
            jnp.int32, (64, 128), 1
        )
        stat_row = lax.broadcasted_iota(jnp.int32, (16, 128), 0)
        for j in range(8):
            chunk = xq * 8 + (pair + turns[j // 2]) % 4 * 2 + j % 2
            send_ref[chunk, :64] = result[j * 64 : (j + 1) * 64]
            line = jnp.where(eye, level[j * 64 : (j + 1) * 64], 0.0)
            line = jnp.sum(line, axis=0, keepdims=True)
            one = line.astype(jnp.bfloat16).astype(jnp.float32)
            two = (line - one).astype(jnp.bfloat16).astype(jnp.float32)
            three = line - one - two
            stats = jnp.where(stat_row == 2, three, 0.0)
            stats = jnp.where(stat_row == 0, one, jnp.where(stat_row == 1, two, stats))
            send_ref[chunk, 64:80] = stats.astype(jnp.bfloat16)

    order = [(3, 0), (2, 0), (1, 0), (0, 0), (3, 1), (2, 1), (1, 1), (3, 2), (2, 2), (3, 3)]
    scores = score(*order[0])
    for now, later in zip(order, order[1:] + [None]):
        ahead = None if later is None else score(*later)
        absorb(*now, scores)
        if now[0] == now[1]:
            finish(now[0])
        scores = ahead


def combine_kernel(recv_ref, out_ref):
    eye = lax.broadcasted_iota(jnp.int32, (64, 128), 0) == lax.broadcasted_iota(
        jnp.int32, (64, 128), 1
    )
    for x in range(4):
        heads = []
        for zp in range(2):
            chunks = [x * 8 + part * 2 + zp for part in range(4)]
            levels = []
            for chunk in chunks:
                stats = recv_ref[chunk, 64:80].astype(jnp.float32)
                levels.append(stats[0:1] + stats[1:2] + stats[2:3])
            top = functools.reduce(jnp.maximum, levels)
            shares = [jnp.exp2(level - top) for level in levels]
            whole = functools.reduce(jnp.add, shares)
            total = None
            for chunk, share in zip(chunks, shares):
                column = jnp.sum(jnp.where(eye, share / whole, 0.0), axis=1, keepdims=True)
                term = recv_ref[chunk, :64].astype(jnp.float32) * column
                total = term if total is None else total + term
            heads.append(total.reshape(8, 8, 128))
        out_ref[:, x * 16 : (x + 1) * 16, :] = jnp.concatenate(heads, axis=1).astype(jnp.bfloat16)


def params():
    return pltpu.CompilerParams(vmem_limit_bytes=40 * 1024 * 1024)


def cost(flops, exps, size):
    return pl.CostEstimate(flops=flops, bytes_accessed=size, transcendentals=exps)


def on_device(queries, text_keyval, visual_keyval, visual_counts):
    owners = math.prod(SIZES)
    following = lax.ppermute(visual_keyval, AXES, [(i, i - 1) for i in range(1, owners)])
    q_chunks, moved, visual, window = pl.pallas_call(
        local_kernel,
        out_shape=(
            jax.ShapeDtypeStruct((8, 64, 128), jnp.bfloat16),
            jax.ShapeDtypeStruct((2048, 128), jnp.bfloat16),
            jax.ShapeDtypeStruct((768, 128), jnp.bfloat16),
            jax.ShapeDtypeStruct((2,), jnp.int32),
        ),
        in_specs=[VMEM] * 4,
        out_specs=(VMEM, VMEM, VMEM, SMEM),
        compiler_params=params(),
        cost_estimate=cost(2 * 2048 * 256 * 128, 0, 3 * 2**20),
        name="local_rows",
    )(
        visual_counts.reshape(2, 128),
        queries,
        text_keyval.reshape(2048, 128),
        visual_keyval.reshape(768, 128),
    )
    send = pl.pallas_call(
        place_kernel,
        out_shape=jax.ShapeDtypeStruct((8, 320, 128), jnp.bfloat16),
        in_specs=[SMEM, VMEM, VMEM, VMEM, VMEM],
        out_specs=VMEM,
        scratch_shapes=[pltpu.VMEM((48 * 3 * 16, 128), jnp.bfloat16)],
        compiler_params=params(),
        cost_estimate=cost(2 * 1536 * 256 * 128, 0, 2**21),
        name="place_rows",
    )(window, q_chunks, moved, visual, following.reshape(768, 128))
    received = lax.all_to_all(send, ("x", "zp"), 0, 0, tiled=True)
    kv = received[:, :256]
    q_mine = received[:, 256:].reshape(512, 128)

    def apart(value, axis):
        turns = [(2 * i + c, 2 * ((i + 1 - 2 * c) % 4) + c) for i in range(4) for c in range(2)]
        return lax.ppermute(value, (*axis, "c"), turns)

    def swap(value):
        return lax.ppermute(value, "c", [(0, 1), (1, 0)])

    q_pair = apart(jnp.concatenate([q_mine, swap(q_mine)], axis=0), ("zh", "k"))
    q_near = q_pair[:512]
    q_far = swap(q_pair[512:])
    q_across = apart(q_near, ("zh", "k"))
    kv_own = jnp.concatenate([kv, swap(kv)], axis=0)
    kv_near = apart(kv_own, ("y",))
    kv_far = swap(kv_near)
    kv_across = apart(kv_near[:8], ("y",))
    q_all = pl.pallas_call(
        scale_kernel,
        out_shape=jax.ShapeDtypeStruct((2048, 256), jnp.bfloat16),
        in_specs=[VMEM] * 4,
        out_specs=VMEM,
        compiler_params=params(),
        cost_estimate=cost(2**20, 0, 2**21),
        name="scale_queries",
    )(q_mine, q_near, q_across, q_far)

    def attend(name, steps, swapped, values, state, weight=4):
        last = name == "attend_d"
        if last:
            out_shape, out_specs = jax.ShapeDtypeStruct((32, 80, 128), jnp.bfloat16), VMEM
        else:
            out_shape = (
                jax.ShapeDtypeStruct((2048, 256), jnp.float32),
                jax.ShapeDtypeStruct((2048, 128), jnp.float32),
            )
            out_specs = (VMEM, VMEM)
        operands = (q_all, *values, *state)
        return pl.pallas_call(
            functools.partial(
                attend_kernel, steps, swapped, len(values) == 1, not state, last
            ),
            out_shape=out_shape,
            in_specs=[VMEM] * len(operands),
            out_specs=out_specs,
            compiler_params=params(),
            cost_estimate=cost(weight * 2621440 * 256, 2621440, 6 * 2**20),
            name=name,
        )(*operands)

    state = attend("attend_a", (0, 0), 0, (kv_own,), ())
    state = attend("attend_b", (3, -2), 0, (kv_near,), state)
    state = attend("attend_c", (1, 2), 1, (kv_far,), state, 16)
    o_send = attend("attend_d", (2, 0), 0, (kv_across, swap(kv_across)), state)
    o_recv = lax.all_to_all(o_send, QUERY_GROUP, 0, 0, tiled=True)
    return pl.pallas_call(
        combine_kernel,
        out_shape=jax.ShapeDtypeStruct((8, 64, 128), jnp.bfloat16),
        in_specs=[VMEM],
        out_specs=VMEM,
        compiler_params=params(),
        cost_estimate=cost(2**20, 4096, 2**20),
        name="combine_parts",
    )(o_recv)


def solution(mesh):
    fine = Mesh(mesh.devices.reshape(SIZES), AXES)
    in_specs = (
        P(AXES, None, None),
        P(AXES, None, None, None),
        P(AXES, None, None, None),
        P(),
    )
    out_specs = P(AXES, None, None)
    return jax.shard_map(
        on_device, mesh=fine, in_specs=in_specs, out_specs=out_specs, check_vma=False
    )
```

```python
import functools
import math

import jax
import jax.numpy as jnp
from jax import lax
from jax.experimental import pallas as pl
from jax.experimental.pallas import tpu as pltpu
from jax.sharding import Mesh, PartitionSpec as P

AXES = ("x", "zh", "y", "k", "zp", "c")
SIZES = (4, 2, 4, 2, 2, 2)
QUERY_GROUP = ("x", "zh", "k", "zp")
NEVER = -1e30
VMEM = pl.BlockSpec(memory_space=pltpu.VMEM)
SMEM = pl.BlockSpec(memory_space=pltpu.SMEM)


def head_order():
    out_row = lax.broadcasted_iota(jnp.int32, (256, 256), 0)
    in_row = lax.broadcasted_iota(jnp.int32, (256, 256), 1)
    moves = jnp.where(in_row == (out_row % 16) * 16 + out_row // 16, 1.0, 0.0)
    return moves.astype(jnp.bfloat16)


def local_kernel(
    counts_ref, q_ref, text_ref, vis_ref, q_out_ref, moved_ref, vis_out_ref, window_ref
):
    owner = 0
    for axis, size in zip(AXES, SIZES):
        owner = owner * size + lax.axis_index(axis)
    counts = counts_ref[...].astype(jnp.float32)
    order = lax.broadcasted_iota(jnp.int32, counts.shape, 0) * 128 + lax.broadcasted_iota(
        jnp.int32, counts.shape, 1
    )
    before = jnp.sum(jnp.where(order < owner, counts, 0.0)).astype(jnp.int32)
    here = jnp.sum(jnp.where(order == owner, counts, 0.0)).astype(jnp.int32)
    window_ref[0] = jnp.clip(before - owner * 48, 0, 47)
    window_ref[1] = here
    for pair in range(4):
        both = q_ref[:, pair * 16 : (pair + 1) * 16, :].astype(jnp.float32)
        for zp in range(2):
            chunk = both[:, zp * 8 : (zp + 1) * 8, :].reshape(64, 128)
            q_out_ref[pair * 2 + zp] = chunk.astype(jnp.bfloat16)
    vis_out_ref[...] = vis_ref[...]
    moves = head_order()
    for part in range(8):
        rows = slice(part * 256, (part + 1) * 256)
        moved_ref[rows] = jnp.dot(
            moves, text_ref[rows], preferred_element_type=jnp.float32
        ).astype(jnp.bfloat16)


def scale_kernel(*refs):
    *q_refs, out_ref = refs
    scale = math.log2(math.e) / math.sqrt(128)
    size = 128 * len(q_refs)
    for xq in range(4):
        sets = [ref[xq * 128 : (xq + 1) * 128] for ref in q_refs]
        scaled = jnp.concatenate(sets, axis=0).astype(jnp.float32) * scale
        high = scaled.astype(jnp.bfloat16)
        low = (scaled - high.astype(jnp.float32)).astype(jnp.bfloat16)
        out_ref[xq * size : (xq + 1) * size] = jnp.concatenate([high, low], axis=1)


def place_kernel(window_ref, q_ref, moved_ref, vis_ref, next_ref, send_ref, stacked):
    send_ref[:, 256:320] = q_ref[...]
    start = window_ref[0]
    here = window_ref[1]
    stacked[0:768] = vis_ref[...]
    stacked[768:1536] = next_ref[...]
    stacked[1536:2304] = jnp.zeros((768, 128), jnp.bfloat16)
    moves = head_order()
    row_within = lax.broadcasted_iota(jnp.int32, (256, 128), 0) % 16
    for part in range(8):
        data = moved_ref[part * 256 : (part + 1) * 256]
        if part < 6:
            first = pl.multiple_of(start * 16 + part * 256, 16)
            window = jnp.dot(moves, stacked[pl.ds(first, 256)], preferred_element_type=jnp.float32)
            data = jnp.where(row_within + part * 16 < here, window, data.astype(jnp.float32))
            data = data.astype(jnp.bfloat16)
        for head in range(8):
            for kind in range(2):
                slab = data[(head * 2 + kind) * 16 : (head * 2 + kind + 1) * 16]
                first_row = kind * 128 + part * 16
                send_ref[head, first_row : first_row + 16] = slab


FIRST_SET = (0, 1, 2)
SECOND_SET = (3,)
ONE_BY_ONE = [
    ((xq,), xk)
    for xq, xk in ((3, 0), (2, 0), (1, 0), (0, 0), (3, 1), (2, 1), (1, 1), (3, 2), (2, 2), (3, 3))
]
STACKED = [((0, 1, 2, 3), 0), ((1, 2, 3), 1), ((2, 3), 2), ((3,), 3)]


def attend_kernel(sets, sources, first, last, *refs):
    refs = list(refs)
    q_refs = [refs.pop(0) for _ in sets]
    kv_refs = []
    for _, _, shared in sources:
        ref = refs.pop(0)
        kv_refs.append([ref.at[0:8], ref.at[8:16]] if shared else [ref, refs.pop(0)])
    states_in = [] if first else [(refs.pop(0), refs.pop(0)) for _ in sets]
    if last:
        (send_ref,) = refs
    else:
        acc_ref, m_ref = refs
    me = {axis: lax.axis_index(axis) for axis in ("zh", "y", "k", "c")}
    pair = me["zh"] * 2 + me["k"]
    every_turn = (0, 3 - 2 * me["c"], 1 + 2 * me["c"], 2)
    turns = [every_turn[group] for groups in sets for group in groups]
    size = 128 * len(turns)
    ones = jnp.ones((512, 128), jnp.bfloat16)
    row = lax.broadcasted_iota(jnp.int32, (size, 128), 0)
    lane = lax.broadcasted_iota(jnp.int32, (size, 128), 1)
    turn = row * 0 + turns[0]
    for j in range(1, len(turns)):
        turn = jnp.where(row // 128 == j, turns[j], turn)
    z = (pair + turn) % 4
    q_dev = (z // 2) * 32 + me["y"] * 8 + (z % 2) * 4 + (row // 64 % 2) * 2 + me["c"]
    reach = q_dev * 128 + 120 + (row % 64) // 8 - lane

    def joined(some_refs, xq):
        found = []
        for groups, ref in zip(sets, some_refs):
            rows = 128 * len(groups)
            found.append(ref[xq * rows : (xq + 1) * rows])
        return found[0] if len(found) == 1 else jnp.concatenate(found, axis=0)

    queries = [joined(q_refs, xq) for xq in range(4)]
    state = [None] * 4
    if not first:
        for xq in range(4):
            acc = joined([acc_in for acc_in, _ in states_in], xq)
            state[xq] = (joined([m_in for _, m_in in states_in], xq), acc)

    def gathered(source, xk, kind):
        found = []
        for kv_ref in kv_refs[source]:
            rows = kv_ref[xk * 2 : xk * 2 + 2, kind * 128 : (kind + 1) * 128]
            found.append(rows.reshape(256, 128))
        return jnp.concatenate(found, axis=0)

    def score(source, xqs, xk):
        keys = gathered(source, xk, 0)
        return lax.dot_general(
            jnp.concatenate([queries[xq] for xq in xqs], axis=0),
            jnp.concatenate([keys, keys], axis=1),
            (((1,), (1,)), ((), ())),
            preferred_element_type=jnp.float32,
        )

    def absorb(source, xqs, xk, scores):
        steps, swapped, _ = sources[source]
        y = (me["y"] + steps[0] + steps[1] * me["c"]) % 4
        weights, maxima = [], []
        for i, xq in enumerate(xqs):
            mine = scores[i * size : (i + 1) * size]
            parts = [mine[:, j * 128 : (j + 1) * 128] for j in range(4)]
            if xk == xq:
                for j in range(4):
                    core = me["c"] if j // 2 == swapped else 1 - me["c"]
                    k_dev = me["zh"] * 32 + y * 8 + me["k"] * 4 + j % 2 * 2 + core
                    parts[j] = jnp.where(reach >= k_dev * 128, parts[j], NEVER)
            top = jnp.max(functools.reduce(jnp.maximum, parts), axis=1, keepdims=True)
            if state[xq] is None:
                new = jnp.broadcast_to(top, (size, 128))
            else:
                new = jnp.maximum(state[xq][0], top)
            maxima.append(new)
            exponents = [jnp.exp2(part - new).astype(jnp.bfloat16) for part in parts]
            weights.append(jnp.concatenate(exponents, axis=1))
        values = gathered(source, xk, 1)
        added = jnp.dot(
            jnp.concatenate(weights, axis=0),
            jnp.concatenate([values, ones], axis=1),
            preferred_element_type=jnp.float32,
        )
        for i, (xq, new) in enumerate(zip(xqs, maxima)):
            acc = added[i * size : (i + 1) * size]
            if state[xq] is not None:
                shrink = jnp.exp2(state[xq][0] - new)
                acc = state[xq][1] * jnp.concatenate([shrink, shrink], axis=1) + acc
            state[xq] = (new, acc)

    def finish(xq):
        maxima, acc = state[xq]
        if not last:
            m_ref[xq * size : (xq + 1) * size] = maxima
            acc_ref[xq * size : (xq + 1) * size] = acc
            return
        totals = acc[:, 128:]
        result = (acc[:, :128] / totals).astype(jnp.bfloat16)
        level = maxima + jnp.log2(totals)
        eye = lax.broadcasted_iota(jnp.int32, (64, 128), 0) == lax.broadcasted_iota(
            jnp.int32, (64, 128), 1
        )
        stat_row = lax.broadcasted_iota(jnp.int32, (16, 128), 0)
        for j in range(8):
            chunk = xq * 8 + (pair + turns[j // 2]) % 4 * 2 + j % 2
            send_ref[chunk, :64] = result[j * 64 : (j + 1) * 64]
            line = jnp.where(eye, level[j * 64 : (j + 1) * 64], 0.0)
            line = jnp.sum(line, axis=0, keepdims=True)
            one = line.astype(jnp.bfloat16).astype(jnp.float32)
            two = (line - one).astype(jnp.bfloat16).astype(jnp.float32)
            three = line - one - two
            stats = jnp.where(stat_row == 2, three, 0.0)
            stats = jnp.where(stat_row == 0, one, jnp.where(stat_row == 1, two, stats))
            send_ref[chunk, 64:80] = stats.astype(jnp.bfloat16)

    order = ONE_BY_ONE if size > 128 else STACKED
    work = [(source, *tile) for source in range(len(sources)) for tile in order]
    scores = score(*work[0])
    for i, (source, xqs, xk) in enumerate(work):
        ahead = score(*work[i + 1]) if i + 1 < len(work) else None
        absorb(source, xqs, xk, scores)
        if source == len(sources) - 1:
            for xq in xqs:
                if xq == xk:
                    finish(xq)
        scores = ahead


def combine_kernel(recv_ref, out_ref):
    eye = lax.broadcasted_iota(jnp.int32, (64, 128), 0) == lax.broadcasted_iota(
        jnp.int32, (64, 128), 1
    )
    for x in range(4):
        heads = []
        for zp in range(2):
            chunks = [x * 8 + part * 2 + zp for part in range(4)]
            levels = []
            for chunk in chunks:
                stats = recv_ref[chunk, 64:80].astype(jnp.float32)
                levels.append(stats[0:1] + stats[1:2] + stats[2:3])
            top = functools.reduce(jnp.maximum, levels)
            shares = [jnp.exp2(level - top) for level in levels]
            whole = functools.reduce(jnp.add, shares)
            total = None
            for chunk, share in zip(chunks, shares):
                column = jnp.sum(jnp.where(eye, share / whole, 0.0), axis=1, keepdims=True)
                term = recv_ref[chunk, :64].astype(jnp.float32) * column
                total = term if total is None else total + term
            heads.append(total.reshape(8, 8, 128))
        out_ref[:, x * 16 : (x + 1) * 16, :] = jnp.concatenate(heads, axis=1).astype(jnp.bfloat16)


def params():
    return pltpu.CompilerParams(vmem_limit_bytes=40 * 1024 * 1024)


def cost(flops, exps, size):
    return pl.CostEstimate(flops=flops, bytes_accessed=size, transcendentals=exps)


def on_device(queries, text_keyval, visual_keyval, visual_counts):
    owners = math.prod(SIZES)
    following = lax.ppermute(visual_keyval, AXES, [(i, i - 1) for i in range(1, owners)])
    q_chunks, moved, visual, window = pl.pallas_call(
        local_kernel,
        out_shape=(
            jax.ShapeDtypeStruct((8, 64, 128), jnp.bfloat16),
            jax.ShapeDtypeStruct((2048, 128), jnp.bfloat16),
            jax.ShapeDtypeStruct((768, 128), jnp.bfloat16),
            jax.ShapeDtypeStruct((2,), jnp.int32),
        ),
        in_specs=[VMEM] * 4,
        out_specs=(VMEM, VMEM, VMEM, SMEM),
        compiler_params=params(),
        cost_estimate=cost(2 * 2048 * 256 * 128, 0, 3 * 2**20),
        name="local_rows",
    )(
        visual_counts.reshape(2, 128),
        queries,
        text_keyval.reshape(2048, 128),
        visual_keyval.reshape(768, 128),
    )
    send = pl.pallas_call(
        place_kernel,
        out_shape=jax.ShapeDtypeStruct((8, 320, 128), jnp.bfloat16),
        in_specs=[SMEM, VMEM, VMEM, VMEM, VMEM],
        out_specs=VMEM,
        scratch_shapes=[pltpu.VMEM((48 * 3 * 16, 128), jnp.bfloat16)],
        compiler_params=params(),
        cost_estimate=cost(2 * 1536 * 256 * 128, 0, 2**21),
        name="place_rows",
    )(window, q_chunks, moved, visual, following.reshape(768, 128))
    received = lax.all_to_all(send, ("x", "zp"), 0, 0, tiled=True)
    kv = received[:, :256]
    q_mine = received[:, 256:].reshape(512, 128)

    def apart(value, axis):
        turns = [(2 * i + c, 2 * ((i + 1 - 2 * c) % 4) + c) for i in range(4) for c in range(2)]
        return lax.ppermute(value, (*axis, "c"), turns)

    def swap(value):
        return lax.ppermute(value, "c", [(0, 1), (1, 0)])

    q_pair = apart(jnp.concatenate([q_mine, swap(q_mine)], axis=0), ("zh", "k"))
    q_near = q_pair[:512]
    q_far = swap(q_pair[512:])
    q_across = apart(q_near, ("zh", "k"))
    kv_own = jnp.concatenate([kv, swap(kv)], axis=0)
    kv_near = apart(kv_own, ("y",))
    def scaled(*values):
        return pl.pallas_call(
            scale_kernel,
            out_shape=jax.ShapeDtypeStruct((512 * len(values), 256), jnp.bfloat16),
            in_specs=[VMEM] * len(values),
            out_specs=VMEM,
            compiler_params=params(),
            cost_estimate=cost(2**20, 0, 2**21),
            name="scale_queries",
        )(*values)

    q_first = scaled(q_mine, q_near, q_far)

    def attend(name, sets, q_sets, sources, values, states, weight=4):
        last = name == "attend_d"
        if last:
            out_shape, out_specs = jax.ShapeDtypeStruct((32, 80, 128), jnp.bfloat16), VMEM
        else:
            rows = 512 * len(sets[0])
            out_shape = (
                jax.ShapeDtypeStruct((rows, 256), jnp.float32),
                jax.ShapeDtypeStruct((rows, 128), jnp.float32),
            )
            out_specs = (VMEM, VMEM)
        operands = (*q_sets, *values, *(part for state in states for part in state))
        return pl.pallas_call(
            functools.partial(attend_kernel, sets, sources, not states, last),
            out_shape=out_shape,
            in_specs=[VMEM] * len(operands),
            out_specs=out_specs,
            compiler_params=params(),
            cost_estimate=cost(weight * 2621440 * 256, 2621440, 6 * 2**20),
            name=name,
        )(*operands)

    own, near, far = ((0, 0), 0, True), ((3, -2), 0, True), ((1, 2), 1, True)
    across = ((2, 0), 0, False)
    one, two = (FIRST_SET,), (SECOND_SET,)
    state = attend("attend_a", one, [q_first], (own,), (kv_own,), [])
    kv_near, state = lax.optimization_barrier((kv_near, state))
    kv_far = swap(kv_near)
    kv_across = apart(kv_near[:8], ("y",))
    state = attend("attend_b", one, [q_first], (near,), (kv_near,), [state])
    state = attend("attend_c", one, [q_first], (far,), (kv_far,), [state], 2)
    q_across, kv_across, state = lax.optimization_barrier((q_across, kv_across, state))
    q_second = scaled(q_across)
    extra = attend(
        "attend_e", two, [q_second], (own, near, far), (kv_own, kv_near, kv_far), [], 16
    )
    o_send = attend(
        "attend_d",
        (FIRST_SET, SECOND_SET),
        [q_first, q_second],
        (across,),
        (kv_across, swap(kv_across)),
        [state, extra],
    )
    o_recv = lax.all_to_all(o_send, QUERY_GROUP, 0, 0, tiled=True)
    return pl.pallas_call(
        combine_kernel,
        out_shape=jax.ShapeDtypeStruct((8, 64, 128), jnp.bfloat16),
        in_specs=[VMEM],
        out_specs=VMEM,
        compiler_params=params(),
        cost_estimate=cost(2**20, 4096, 2**20),
        name="combine_parts",
    )(o_recv)


def solution(mesh):
    fine = Mesh(mesh.devices.reshape(SIZES), AXES)
    in_specs = (
        P(AXES, None, None),
        P(AXES, None, None, None),
        P(AXES, None, None, None),
        P(),
    )
    out_specs = P(AXES, None, None)
    return jax.shard_map(
        on_device, mesh=fine, in_specs=in_specs, out_specs=out_specs, check_vma=False
    )
```

```python
import functools
import math

import jax
import jax.numpy as jnp
from jax import lax
from jax.experimental import pallas as pl
from jax.experimental.pallas import tpu as pltpu
from jax.sharding import Mesh, PartitionSpec as P

AXES = ("x", "zh", "y", "k", "zp", "c")
SIZES = (4, 2, 4, 2, 2, 2)
QUERY_GROUP = ("x", "zh", "k", "zp")
NEVER = -1e30
VMEM = pl.BlockSpec(memory_space=pltpu.VMEM)
SMEM = pl.BlockSpec(memory_space=pltpu.SMEM)


def head_order():
    out_row = lax.broadcasted_iota(jnp.int32, (256, 256), 0)
    in_row = lax.broadcasted_iota(jnp.int32, (256, 256), 1)
    moves = jnp.where(in_row == (out_row % 16) * 16 + out_row // 16, 1.0, 0.0)
    return moves.astype(jnp.bfloat16)


def local_kernel(
    counts_ref, q_ref, text_ref, vis_ref, q_out_ref, moved_ref, vis_out_ref, window_ref
):
    owner = 0
    for axis, size in zip(AXES, SIZES):
        owner = owner * size + lax.axis_index(axis)
    counts = counts_ref[...].astype(jnp.float32)
    order = lax.broadcasted_iota(jnp.int32, counts.shape, 0) * 128 + lax.broadcasted_iota(
        jnp.int32, counts.shape, 1
    )
    before = jnp.sum(jnp.where(order < owner, counts, 0.0)).astype(jnp.int32)
    here = jnp.sum(jnp.where(order == owner, counts, 0.0)).astype(jnp.int32)
    window_ref[0] = jnp.clip(before - owner * 48, 0, 47)
    window_ref[1] = here
    for pair in range(4):
        both = q_ref[:, pair * 16 : (pair + 1) * 16, :].astype(jnp.float32)
        for zp in range(2):
            chunk = both[:, zp * 8 : (zp + 1) * 8, :].reshape(64, 128)
            q_out_ref[pair * 2 + zp] = chunk.astype(jnp.bfloat16)
    vis_out_ref[...] = vis_ref[...]
    moves = head_order()
    for part in range(8):
        rows = slice(part * 256, (part + 1) * 256)
        moved_ref[rows] = jnp.dot(
            moves, text_ref[rows], preferred_element_type=jnp.float32
        ).astype(jnp.bfloat16)


def scale_kernel(*refs):
    *q_refs, out_ref = refs
    scale = math.log2(math.e) / math.sqrt(128)
    size = 128 * len(q_refs)
    for xq in range(4):
        sets = [ref[xq * 128 : (xq + 1) * 128] for ref in q_refs]
        scaled = jnp.concatenate(sets, axis=0).astype(jnp.float32) * scale
        high = scaled.astype(jnp.bfloat16)
        low = (scaled - high.astype(jnp.float32)).astype(jnp.bfloat16)
        out_ref[xq * size : (xq + 1) * size] = jnp.concatenate([high, low], axis=1)


def place_kernel(window_ref, q_ref, moved_ref, vis_ref, next_ref, send_ref, stacked):
    send_ref[:, 256:320] = q_ref[...]
    start = window_ref[0]
    here = window_ref[1]
    stacked[0:768] = vis_ref[...]
    stacked[768:1536] = next_ref[...]
    stacked[1536:2304] = jnp.zeros((768, 128), jnp.bfloat16)
    moves = head_order()
    row_within = lax.broadcasted_iota(jnp.int32, (256, 128), 0) % 16
    for part in range(8):
        data = moved_ref[part * 256 : (part + 1) * 256]
        if part < 6:
            first = pl.multiple_of(start * 16 + part * 256, 16)
            window = jnp.dot(moves, stacked[pl.ds(first, 256)], preferred_element_type=jnp.float32)
            data = jnp.where(row_within + part * 16 < here, window, data.astype(jnp.float32))
            data = data.astype(jnp.bfloat16)
        for head in range(8):
            for kind in range(2):
                slab = data[(head * 2 + kind) * 16 : (head * 2 + kind + 1) * 16]
                first_row = kind * 128 + part * 16
                send_ref[head, first_row : first_row + 16] = slab


FIRST_SET = (0, 1, 2)
SECOND_SET = (3,)
ONE_BY_ONE = [
    ((xq,), xk)
    for xq, xk in ((3, 0), (2, 0), (1, 0), (0, 0), (3, 1), (2, 1), (1, 1), (3, 2), (2, 2), (3, 3))
]
STACKED = [((0, 1, 2, 3), 0), ((1, 2, 3), 1), ((2, 3), 2), ((3,), 3)]


def attend_kernel(sets, sources, first, last, *refs):
    refs = list(refs)
    q_refs = [refs.pop(0) for _ in sets]
    kv_refs = []
    for _, _, shared in sources:
        ref = refs.pop(0)
        kv_refs.append([ref.at[0:8], ref.at[8:16]] if shared else [ref, refs.pop(0)])
    states_in = [] if first else [(refs.pop(0), refs.pop(0)) for _ in sets]
    if last:
        (send_ref,) = refs
    else:
        acc_ref, m_ref = refs
    me = {axis: lax.axis_index(axis) for axis in ("zh", "y", "k", "c")}
    pair = me["zh"] * 2 + me["k"]
    every_turn = (0, 3 - 2 * me["c"], 1 + 2 * me["c"], 2)
    turns = [every_turn[group] for groups in sets for group in groups]
    size = 128 * len(turns)
    ones = jnp.ones((512, 128), jnp.bfloat16)
    row = lax.broadcasted_iota(jnp.int32, (size, 128), 0)
    lane = lax.broadcasted_iota(jnp.int32, (size, 128), 1)
    turn = row * 0 + turns[0]
    for j in range(1, len(turns)):
        turn = jnp.where(row // 128 == j, turns[j], turn)
    z = (pair + turn) % 4
    q_dev = (z // 2) * 32 + me["y"] * 8 + (z % 2) * 4 + (row // 64 % 2) * 2 + me["c"]
    reach = q_dev * 128 + 120 + (row % 64) // 8 - lane

    def joined(some_refs, xq):
        found = []
        for groups, ref in zip(sets, some_refs):
            rows = 128 * len(groups)
            found.append(ref[xq * rows : (xq + 1) * rows])
        return found[0] if len(found) == 1 else jnp.concatenate(found, axis=0)

    queries = [joined(q_refs, xq) for xq in range(4)]
    state = [None] * 4
    if not first:
        for xq in range(4):
            acc = joined([acc_in for acc_in, _ in states_in], xq)
            state[xq] = (joined([m_in for _, m_in in states_in], xq), acc)

    def gathered(source, xk, kind):
        found = []
        for kv_ref in kv_refs[source]:
            rows = kv_ref[xk * 2 : xk * 2 + 2, kind * 128 : (kind + 1) * 128]
            found.append(rows.reshape(256, 128))
        return jnp.concatenate(found, axis=0)

    def score(source, xqs, xk):
        keys = gathered(source, xk, 0)
        return lax.dot_general(
            jnp.concatenate([queries[xq] for xq in xqs], axis=0),
            jnp.concatenate([keys, keys], axis=1),
            (((1,), (1,)), ((), ())),
            preferred_element_type=jnp.float32,
        )

    def absorb(source, xqs, xk, scores):
        steps, swapped, _ = sources[source]
        y = (me["y"] + steps[0] + steps[1] * me["c"]) % 4
        weights, maxima = [], []
        for i, xq in enumerate(xqs):
            mine = scores[i * size : (i + 1) * size]
            parts = [mine[:, j * 128 : (j + 1) * 128] for j in range(4)]
            if xk == xq:
                for j in range(4):
                    core = me["c"] if j // 2 == swapped else 1 - me["c"]
                    k_dev = me["zh"] * 32 + y * 8 + me["k"] * 4 + j % 2 * 2 + core
                    parts[j] = jnp.where(reach >= k_dev * 128, parts[j], NEVER)
            top = jnp.max(functools.reduce(jnp.maximum, parts), axis=1, keepdims=True)
            if state[xq] is None:
                new = jnp.broadcast_to(top, (size, 128))
            else:
                new = jnp.maximum(state[xq][0], top)
            maxima.append(new)
            exponents = [jnp.exp2(part - new).astype(jnp.bfloat16) for part in parts]
            weights.append(jnp.concatenate(exponents, axis=1))
        values = gathered(source, xk, 1)
        added = jnp.dot(
            jnp.concatenate(weights, axis=0),
            jnp.concatenate([values, ones], axis=1),
            preferred_element_type=jnp.float32,
        )
        for i, (xq, new) in enumerate(zip(xqs, maxima)):
            acc = added[i * size : (i + 1) * size]
            if state[xq] is not None:
                shrink = jnp.exp2(state[xq][0] - new)
                acc = state[xq][1] * jnp.concatenate([shrink, shrink], axis=1) + acc
            state[xq] = (new, acc)

    def finish(xq):
        maxima, acc = state[xq]
        if not last:
            m_ref[xq * size : (xq + 1) * size] = maxima
            acc_ref[xq * size : (xq + 1) * size] = acc
            return
        totals = acc[:, 128:]
        result = (acc[:, :128] / totals).astype(jnp.bfloat16)
        level = maxima + jnp.log2(totals)
        eye = lax.broadcasted_iota(jnp.int32, (64, 128), 0) == lax.broadcasted_iota(
            jnp.int32, (64, 128), 1
        )
        stat_row = lax.broadcasted_iota(jnp.int32, (16, 128), 0)
        for j in range(8):
            chunk = xq * 8 + (pair + turns[j // 2]) % 4 * 2 + j % 2
            send_ref[chunk, :64] = result[j * 64 : (j + 1) * 64]
            line = jnp.where(eye, level[j * 64 : (j + 1) * 64], 0.0)
            line = jnp.sum(line, axis=0, keepdims=True)
            one = line.astype(jnp.bfloat16).astype(jnp.float32)
            two = (line - one).astype(jnp.bfloat16).astype(jnp.float32)
            three = line - one - two
            stats = jnp.where(stat_row == 2, three, 0.0)
            stats = jnp.where(stat_row == 0, one, jnp.where(stat_row == 1, two, stats))
            send_ref[chunk, 64:80] = stats.astype(jnp.bfloat16)

    order = ONE_BY_ONE if size > 128 else STACKED
    work = [(source, *tile) for source in range(len(sources)) for tile in order]
    scores = score(*work[0])
    for i, (source, xqs, xk) in enumerate(work):
        ahead = score(*work[i + 1]) if i + 1 < len(work) else None
        absorb(source, xqs, xk, scores)
        if source == len(sources) - 1:
            for xq in xqs:
                if xq == xk:
                    finish(xq)
        scores = ahead


def combine_kernel(recv_ref, out_ref):
    row = lax.broadcasted_iota(jnp.int32, (64, 256), 0)
    lane = lax.broadcasted_iota(jnp.int32, (64, 256), 1)
    diagonal = lane % 64 == row
    for x in range(4):
        heads = []
        for zp in range(2):
            chunks = [x * 8 + part * 2 + zp for part in range(4)]
            levels = []
            for chunk in chunks:
                stats = recv_ref[chunk, 64:80].astype(jnp.float32)
                levels.append(stats[0:1] + stats[1:2] + stats[2:3])
            top = functools.reduce(jnp.maximum, levels)
            shares = [jnp.exp2(level - top) for level in levels]
            whole = functools.reduce(jnp.add, shares)
            line = jnp.concatenate([(share / whole)[:, :64] for share in shares], axis=1)
            weights = jnp.where(diagonal, line, 0.0)
            high = weights.astype(jnp.bfloat16)
            low = (weights - high.astype(jnp.float32)).astype(jnp.bfloat16)
            data = jnp.concatenate([recv_ref[chunk, :64] for chunk in chunks], axis=0)
            total = jnp.dot(
                jnp.concatenate([high, low], axis=1),
                jnp.concatenate([data, data], axis=0),
                preferred_element_type=jnp.float32,
            )
            heads.append(total.reshape(8, 8, 128))
        out_ref[:, x * 16 : (x + 1) * 16, :] = jnp.concatenate(heads, axis=1).astype(jnp.bfloat16)


def params():
    return pltpu.CompilerParams(vmem_limit_bytes=40 * 1024 * 1024)


def cost(flops, exps, size):
    return pl.CostEstimate(flops=flops, bytes_accessed=size, transcendentals=exps)


def on_device(queries, text_keyval, visual_keyval, visual_counts):
    owners = math.prod(SIZES)
    following = lax.ppermute(visual_keyval, AXES, [(i, i - 1) for i in range(1, owners)])
    q_chunks, moved, visual, window = pl.pallas_call(
        local_kernel,
        out_shape=(
            jax.ShapeDtypeStruct((8, 64, 128), jnp.bfloat16),
            jax.ShapeDtypeStruct((2048, 128), jnp.bfloat16),
            jax.ShapeDtypeStruct((768, 128), jnp.bfloat16),
            jax.ShapeDtypeStruct((2,), jnp.int32),
        ),
        in_specs=[VMEM] * 4,
        out_specs=(VMEM, VMEM, VMEM, SMEM),
        compiler_params=params(),
        cost_estimate=cost(2 * 2048 * 256 * 128, 0, 3 * 2**20),
        name="local_rows",
    )(
        visual_counts.reshape(2, 128),
        queries,
        text_keyval.reshape(2048, 128),
        visual_keyval.reshape(768, 128),
    )
    send = pl.pallas_call(
        place_kernel,
        out_shape=jax.ShapeDtypeStruct((8, 320, 128), jnp.bfloat16),
        in_specs=[SMEM, VMEM, VMEM, VMEM, VMEM],
        out_specs=VMEM,
        scratch_shapes=[pltpu.VMEM((48 * 3 * 16, 128), jnp.bfloat16)],
        compiler_params=params(),
        cost_estimate=cost(2 * 1536 * 256 * 128, 0, 2**21),
        name="place_rows",
    )(window, q_chunks, moved, visual, following.reshape(768, 128))
    received = lax.all_to_all(send, ("x", "zp"), 0, 0, tiled=True)
    kv = received[:, :256]
    q_mine = received[:, 256:].reshape(512, 128)

    def apart(value, axis):
        turns = [(2 * i + c, 2 * ((i + 1 - 2 * c) % 4) + c) for i in range(4) for c in range(2)]
        return lax.ppermute(value, (*axis, "c"), turns)

    def swap(value):
        return lax.ppermute(value, "c", [(0, 1), (1, 0)])

    q_pair = apart(jnp.concatenate([q_mine, swap(q_mine)], axis=0), ("zh", "k"))
    q_near = q_pair[:512]
    q_far = swap(q_pair[512:])
    q_across = apart(q_near, ("zh", "k"))
    kv_own = jnp.concatenate([kv, swap(kv)], axis=0)
    kv_near = apart(kv_own, ("y",))
    def scaled(*values):
        return pl.pallas_call(
            scale_kernel,
            out_shape=jax.ShapeDtypeStruct((512 * len(values), 256), jnp.bfloat16),
            in_specs=[VMEM] * len(values),
            out_specs=VMEM,
            compiler_params=params(),
            cost_estimate=cost(2**20, 0, 2**21),
            name="scale_queries",
        )(*values)

    q_first = scaled(q_mine, q_near, q_far)

    def attend(name, sets, q_sets, sources, values, states, weight=4):
        last = name == "attend_d"
        if last:
            out_shape, out_specs = jax.ShapeDtypeStruct((32, 80, 128), jnp.bfloat16), VMEM
        else:
            rows = 512 * len(sets[0])
            out_shape = (
                jax.ShapeDtypeStruct((rows, 256), jnp.float32),
                jax.ShapeDtypeStruct((rows, 128), jnp.float32),
            )
            out_specs = (VMEM, VMEM)
        operands = (*q_sets, *values, *(part for state in states for part in state))
        return pl.pallas_call(
            functools.partial(attend_kernel, sets, sources, not states, last),
            out_shape=out_shape,
            in_specs=[VMEM] * len(operands),
            out_specs=out_specs,
            compiler_params=params(),
            cost_estimate=cost(weight * 2621440 * 256, 2621440, 6 * 2**20),
            name=name,
        )(*operands)

    own, near, far = ((0, 0), 0, True), ((3, -2), 0, True), ((1, 2), 1, True)
    across = ((2, 0), 0, False)
    one, two = (FIRST_SET,), (SECOND_SET,)
    state = attend("attend_a", one, [q_first], (own,), (kv_own,), [])
    kv_near, state = lax.optimization_barrier((kv_near, state))
    kv_far = swap(kv_near)
    kv_across = apart(kv_near[:8], ("y",))
    state = attend("attend_b", one, [q_first], (near,), (kv_near,), [state])
    state = attend("attend_c", one, [q_first], (far,), (kv_far,), [state], 2)
    q_across, kv_across, state = lax.optimization_barrier((q_across, kv_across, state))
    q_second = scaled(q_across)
    extra = attend(
        "attend_e", two, [q_second], (own, near, far), (kv_own, kv_near, kv_far), [], 16
    )
    o_send = attend(
        "attend_d",
        (FIRST_SET, SECOND_SET),
        [q_first, q_second],
        (across,),
        (kv_across, swap(kv_across)),
        [state, extra],
    )
    o_recv = lax.all_to_all(o_send, QUERY_GROUP, 0, 0, tiled=True)
    return pl.pallas_call(
        combine_kernel,
        out_shape=jax.ShapeDtypeStruct((8, 64, 128), jnp.bfloat16),
        in_specs=[VMEM],
        out_specs=VMEM,
        compiler_params=params(),
        cost_estimate=cost(2**20, 4096, 2**20),
        name="combine_parts",
    )(o_recv)


def solution(mesh):
    fine = Mesh(mesh.devices.reshape(SIZES), AXES)
    in_specs = (
        P(AXES, None, None),
        P(AXES, None, None, None),
        P(AXES, None, None, None),
        P(),
    )
    out_specs = P(AXES, None, None)
    return jax.shard_map(
        on_device, mesh=fine, in_specs=in_specs, out_specs=out_specs, check_vma=False
    )
```
